32 devices in a mesh: grp: 4 (over z), dev: 8 (over y, x, core).
Axes of the slice: x: 2, y: 2, z: 4, core: 2. Of those that a mesh axis runs over, the one named last changes fastest.
Arguments:
- orbitals: bfloat16 [4, 8, 64, 2, 2304], P('grp', 'dev'), may hold values from -6 to 6
- potential: bfloat16 [8, 2304], P('dev'), may hold values from -4 to 4
- counts: int32 [4, 8], P('grp'), may hold values from 16 to 64, as said below
- parity: int32 [4, 8], P('grp', 'dev'), may hold values 0 or 1
Outputs:
- density: float32 [8, 1, 2304], P('dev', None, 'grp')
- filtered: bfloat16 [4, 8, 64, 2, 2304], P('grp', 'dev')
The draws below stay inside these ranges and needn't reach their ends.
Inputs may be any that keep to these rules, and one draw needn't show every extreme that they name: In each row of 8 fragments the counts sum to 224, and some fragment of every row holds 64 orbitals and some holds 16.
All inputs are finite; a program needn't handle non-finite values. No bound on the sum of `parity` on one device may be relied on, other than what follows from the above.
Results may differ from the reference program's by a relative error of at most 0.0026.
Values may be sent and summed in bfloat16 or wider, within the bound.
No kernel may reach another device: no remote copies, remote signals or barrier semaphores. Data moves between devices by JAX's collectives and lax.ppermute only.
A program may use at most 64 MiB of HBM per device.

```python
import jax
import jax.numpy as jnp
from jax import lax

MAXORB = 64
MINORB = 16
DEGREE = 8
BX = 1
BY = 48
BZ = 48
N_GRP = 4
N_DEV = 8


def draw_counts(key, part):
    spread = MAXORB - MINORB
    quads = N_DEV // 4

    def one_group(group_key):
        key_order, key_cuts = jax.random.split(group_key)
        order = jax.random.permutation(key_order, N_DEV)
        cuts = jnp.sort(jax.random.randint(key_cuts, (quads, 3), 0, spread + 1), axis=1)
        cuts = jnp.where(jnp.arange(quads)[:, None] == 0, 0, cuts)
        edges = jnp.concatenate([jnp.zeros((quads, 1), jnp.int32), cuts.astype(jnp.int32), jnp.full((quads, 1), spread, jnp.int32)], 1)
        pieces = (edges[:, 1:] - edges[:, :-1]).reshape(-1)
        values = MINORB + pieces
        return values[jnp.argsort(order)].astype(jnp.int32)
    group_keys = jax.random.split(jax.random.fold_in(key, 17), N_GRP)
    return jax.vmap(one_group)(group_keys)


def place_ends(array, stream_key, smallest, top_value):
    longest = array.shape.index(max(array.shape))
    spots = []
    for shift in (0, 1):
        where = [jax.random.randint(jax.random.fold_in(stream_key, axis), (), 0, length) for axis, length in enumerate(array.shape)]
        where[longest] = (where[longest] + shift) % array.shape[longest]
        spots.append(tuple(where))
    return array.at[spots[0]].set(smallest).at[spots[1]].set(top_value)


def steps_of(rng, shape, shards, low, top_value):
    def one(position, shards_of):
        heights = jax.random.uniform(jax.random.fold_in(jax.random.fold_in(rng, 6), position), (shards_of,), jnp.float32, low / len(shards), top_value / len(shards))
        return jnp.repeat(jnp.exp(heights), shape[position] // shards_of).reshape((-1,) + (1,) * (len(shape) - position - 1))

    factor_of = one(*shards[0])
    for cut in shards[1:]:
        factor_of = factor_of * one(*cut)
    return factor_of


def bell_draw(key, shape, scale, bound, cuts=(), kind=jnp.bfloat16):
    factor_of = steps_of(key, shape, cuts, -0.22, 0.18) if cuts else 1.0
    values = jax.random.normal(key, shape, jnp.float32) * scale * factor_of
    return jnp.minimum(jnp.maximum(values, -bound), bound).astype(kind)


def setup_inputs(seed: int = 0) -> dict:
    keys = jax.random.split(jax.random.key(seed), 5)
    orbitals = bell_draw(keys[0], (N_GRP, N_DEV, MAXORB, 2 * BX, BY * BZ), 1.0, 6.0, ((0, 4), (1, 8)))
    potential = bell_draw(keys[1], (N_DEV * BX, BY * BZ), 1.0, 4.0, ((0, 8),))
    counts = draw_counts(jax.random.fold_in(keys[4], 71), 0)
    parity = place_ends((jax.random.randint(keys[3], (N_GRP, N_DEV), 0, 2) < 1).astype(jnp.int32), jax.random.fold_in(keys[3], 1), 0, 1)
    return {"orbitals": orbitals, "potential": potential, "counts": counts, "parity": parity}


filter_centre = 9.0
filter_half = 7.0

def beside_sum(field):
    edge_x = jnp.zeros_like(field[:, :1])
    along_x = jnp.concatenate([field[:, 1:], edge_x], 1) + jnp.concatenate([edge_x, field[:, :-1]], 1)
    edge_y = jnp.zeros_like(field[:, :, :BZ])
    along_y = jnp.concatenate([field[:, :, BZ:], edge_y], 2) + jnp.concatenate([edge_y, field[:, :, :-BZ]], 2)
    edge_z = jnp.zeros_like(field[:, :, :1])
    upper = jnp.concatenate([field[:, :, 1:], edge_z], 2)
    lower = jnp.concatenate([edge_z, field[:, :, :-1]], 2)
    z_index = jnp.arange(field.shape[2]) % BZ
    along_z = jnp.where(z_index == BZ - 1, 0.0, upper) + jnp.where(z_index == 0, 0.0, lower)
    return along_x + along_y + along_z

def step_map(field, patches):
    return (6.0 * field - beside_sum(field) + patches * field - filter_centre * field) / filter_half

def chebyshev_rows(orbital_rows, patches):
    previous = orbital_rows.astype(jnp.float32)
    current = step_map(previous, patches)
    for degree_step in range(DEGREE - 1):
        previous, current = (current, 2.0 * step_map(current, patches) - previous)
    mean_square = lax.optimization_barrier(jnp.mean(current * current, axis=(1, 2), keepdims=True))
    return (current * lax.rsqrt(mean_square + 1e-06)).astype(jnp.bfloat16)

def reference(orbitals, potential, counts, parity):
    blocks = potential.astype(jnp.float32).reshape(N_DEV, BX, BY * BZ)
    patches = jnp.concatenate([blocks, jnp.roll(blocks, -1, axis=0)], axis=1)
    patches = jnp.tile(patches, (N_GRP, 1, 1))
    slot_ids = jnp.arange(MAXORB, dtype=jnp.int32)

    def fragment(inputs):
        orbital_rows, own_patch, my_count, parity_bit = inputs
        result = chebyshev_rows(orbital_rows, own_patch[None])
        result = jnp.where((slot_ids < my_count)[:, None, None], result, jnp.zeros((), jnp.bfloat16))
        squares = result.astype(jnp.float32)
        density_part = lax.optimization_barrier(jnp.sum(squares * squares, axis=0)) * ((1.0 - 2.0 * parity_bit.astype(jnp.float32)) / MAXORB)
        return (result, density_part)
    stacked = orbitals.reshape(N_GRP * N_DEV, MAXORB, 2 * BX, BY * BZ)
    results, parts = lax.map(fragment, (stacked, patches, counts.reshape(-1), parity.reshape(-1)))
    totals = lax.optimization_barrier(jnp.sum(parts.reshape(N_GRP, N_DEV, 2, BX, BY * BZ), axis=0))
    density = totals[:, 0] + jnp.roll(totals[:, 1], 1, axis=0)
    return (density, results.reshape(orbitals.shape))
```

```python
import functools

import jax
import jax.numpy as jnp
from jax import lax
from jax.experimental import pallas as pl
from jax.experimental.pallas import tpu as pltpu
from jax.sharding import PartitionSpec as P

DEGREE = 8
BZ = 48
SUB = 8

filter_centre = 9.0
filter_half = 7.0


def filter_kernel(scalars, orbital_ref, patch_ref, filtered_ref, density_ref, plain, diagonal, one, two):
    rows, cells = orbital_ref.shape
    slots = rows // 2
    chunk = 256
    strips = BZ // SUB
    planes_y = cells // BZ
    count, parity = scalars[0], scalars[1]

    eye = (
        lax.broadcasted_iota(jnp.int32, (chunk, chunk), 0)
        == lax.broadcasted_iota(jnp.int32, (chunk, chunk), 1)
    ).astype(jnp.float32).astype(jnp.bfloat16)
    across = (((1,), (1,)), ((), ()))

    for start in range(0, cells, chunk):
        plain[pl.ds(start, chunk), :] = lax.dot_general(
            eye, orbital_ref[:, start : start + chunk], across, preferred_element_type=jnp.float32
        )
        near = jnp.broadcast_to(patch_ref[0:1, start : start + chunk], (slots, chunk))
        far = jnp.broadcast_to(patch_ref[1:2, start : start + chunk], (slots, chunk))
        potential = lax.dot_general(
            eye, jnp.concatenate([near, far], 0), across, preferred_element_type=jnp.float32
        )
        diagonal[pl.ds(start, chunk), :] = potential + (6.0 - filter_centre)
    zeros = jnp.zeros((BZ, rows), jnp.float32)
    plain[pl.ds(cells, BZ), :] = zeros
    one[pl.ds(cells, BZ), :] = zeros
    two[pl.ds(cells, BZ), :] = zeros

    sub_ids = lax.broadcasted_iota(jnp.int32, (SUB, rows), 0)

    def strided(ref, y):
        return jnp.concatenate(
            [ref[pl.ds(y * BZ + zi, SUB, stride=strips), :] for zi in range(strips)], 0
        )

    def packed(ref, y):
        return ref[pl.ds(y * BZ, BZ), :]

    def around(before, here, after):
        up = jnp.where(sub_ids == 0, 0.0, pltpu.roll(here[BZ - SUB :], 1, 0))
        down = jnp.where(sub_ids == SUB - 1, 0.0, pltpu.roll(here[:SUB], SUB - 1, 0))
        along_z = jnp.concatenate([up, here[: BZ - SUB]], 0) + jnp.concatenate([here[SUB:], down], 0)
        return along_z + (before + after) + pltpu.roll(here, slots, 1)

    def sweep(load, finish):
        def body(y, carry):
            before, here = carry
            after = load(y + 1)
            finish(y, here, around(before, here, after))
            return here, after

        lax.fori_loop(0, planes_y, body, (zeros, load(0)), unroll=4)

    def first(y, here, beside):
        factor = strided(diagonal, y)
        one[pl.ds(y * BZ, BZ), :] = (factor * here - beside) * (1.0 / filter_half)
        two[pl.ds(y * BZ, BZ), :] = here

    sweep(functools.partial(strided, plain), first)

    scale = 2.0 / filter_half

    def later(source, target):
        def finish(y, here, beside):
            factor = strided(diagonal, y)
            target[pl.ds(y * BZ, BZ), :] = (factor * here - beside) * scale - packed(target, y)

        sweep(functools.partial(packed, source), finish)

    def pair(_, carry):
        later(one, two)
        later(two, one)
        return carry

    lax.fori_loop(0, (DEGREE - 2) // 2, pair, 0)

    def last_body(y, carry):
        before, here, total = carry
        after = packed(one, y + 1)
        beside = around(before, here, after)
        value = (strided(diagonal, y) * here - beside) * scale - packed(two, y)
        for zi in range(strips):
            plain[pl.ds(y * BZ + zi, SUB, stride=strips), :] = value[zi * SUB : (zi + 1) * SUB]
        return here, after, total + value * value

    _, _, total = lax.fori_loop(0, planes_y, last_body, (zeros, packed(one, 0), zeros), unroll=4)
    lane_sum = jnp.sum(total, axis=0, keepdims=True)
    lane_sum = jnp.broadcast_to(lane_sum, (SUB, rows))
    mean_square = (lane_sum + pltpu.roll(lane_sum, slots, 1)) * (1.0 / (2 * cells))
    slot_ids = lax.broadcasted_iota(jnp.int32, (SUB, rows), 1) % slots
    factor = jnp.where(slot_ids < count, lax.rsqrt(mean_square + 1e-06), 0.0)[:1]
    signed = (1.0 - 2.0 * parity.astype(jnp.float32)) / slots

    for start in range(0, cells, chunk):
        rounded = (plain[pl.ds(start, chunk), :] * factor).astype(jnp.bfloat16)
        turned = lax.dot_general(
            eye[:rows, :rows], rounded, across, preferred_element_type=jnp.float32
        )
        filtered_ref[:, start : start + chunk] = turned.astype(jnp.bfloat16)
        squares = turned * turned
        density_ref[0:1, start : start + chunk] = jnp.sum(squares[:slots], axis=0, keepdims=True) * signed
        density_ref[1:2, start : start + chunk] = jnp.sum(squares[slots:], axis=0, keepdims=True) * signed


def filter_box(scalars, orbital_rows, patch):
    rows, cells = orbital_rows.shape
    padded = pltpu.VMEM((cells + BZ, rows), jnp.float32)
    return pl.pallas_call(
        filter_kernel,
        out_shape=(
            jax.ShapeDtypeStruct((rows, cells), jnp.bfloat16),
            jax.ShapeDtypeStruct((2, cells), jnp.float32),
        ),
        in_specs=[
            pl.BlockSpec(memory_space=pltpu.SMEM),
            pl.BlockSpec(memory_space=pltpu.VMEM),
            pl.BlockSpec(memory_space=pltpu.VMEM),
        ],
        out_specs=(
            pl.BlockSpec(memory_space=pltpu.VMEM),
            pl.BlockSpec(memory_space=pltpu.VMEM),
        ),
        scratch_shapes=[padded, pltpu.VMEM((cells, rows), jnp.float32), padded, padded],
        compiler_params=pltpu.CompilerParams(vmem_limit_bytes=16 * 2**20),
        name="filter_box",
    )(scalars, orbital_rows, patch)


def sum_over(part, axis):
    size = lax.axis_size(axis)
    if size & (size - 1):
        return lax.psum_scatter(part, axis, scatter_dimension=0, tiled=True)
    me = lax.axis_index(axis)
    span = size // 2
    while span:
        halves = part.reshape(2, -1)
        mine = (me // span) % 2
        kept = jnp.where(mine == 0, halves[0], halves[1])
        sent = jnp.where(mine == 0, halves[1], halves[0])
        part = kept + lax.ppermute(sent, axis, [(i, i ^ span) for i in range(size)])
        span //= 2
    return part


def on_device(orbitals, potential, counts, parity):
    group_size = lax.axis_size("dev")
    me = lax.axis_index("dev")
    slots, _, cells = orbitals.shape[2:]
    following = lax.ppermute(potential, "dev", [((i + 1) % group_size, i) for i in range(group_size)])
    patch = jnp.concatenate([potential, following], 0)
    orbital_rows = jnp.swapaxes(orbitals[0, 0], 0, 1).reshape(2 * slots, cells)
    count = lax.dynamic_index_in_dim(counts[0], me, 0, keepdims=False)
    scalars = jnp.stack([count, parity[0, 0]])
    filtered_rows, halves = filter_box(scalars, orbital_rows, patch)
    carried = lax.ppermute(halves[1], "dev", [(i, (i + 1) % group_size) for i in range(group_size)])
    density = sum_over(halves[0] + carried, "grp")
    filtered = jnp.swapaxes(filtered_rows.reshape(2, slots, cells), 0, 1)
    return density[None, None], filtered[None, None]


def solution(mesh):
    placed = (P("grp", "dev", None, None, None), P("dev", None), P("grp", None), P("grp", "dev"))
    return jax.shard_map(
        on_device,
        mesh=mesh,
        in_specs=placed,
        out_specs=(P("dev", None, "grp"), P("grp", "dev", None, None, None)),
        check_vma=False,
    )
```

```python
import functools
import math

import jax
import jax.numpy as jnp
from jax import lax
from jax.experimental import pallas as pl
from jax.experimental.pallas import tpu as pltpu
from jax.sharding import PartitionSpec as P

DEGREE = 8
BZ = 48
SUB = 8
CHUNK = 256

filter_centre = 9.0
filter_half = 7.0

across = (((1,), (1,)), ((), ()))


def leja_roots():
    rest = [math.cos((2 * j - 1) * math.pi / (2 * DEGREE)) for j in range(1, DEGREE + 1)]
    order = [rest.pop(0)]
    while rest:
        best = max(rest, key=lambda root: sum(math.log(abs(root - other)) for other in order))
        rest.remove(best)
        order.append(best)
    return order


SHIFTS = [filter_half * root for root in leja_roots()]
LEADING = 2.0 ** (DEGREE - 1) / filter_half**DEGREE


def identity(size):
    down = lax.broadcasted_iota(jnp.int32, (size, size), 0)
    along = lax.broadcasted_iota(jnp.int32, (size, size), 1)
    return (down == along).astype(jnp.float32).astype(jnp.bfloat16)


def turn_kernel(orbital_ref, plain):
    eye = identity(CHUNK)
    for start in range(0, orbital_ref.shape[1], CHUNK):
        plain[start : start + CHUNK, :] = lax.dot_general(
            eye, orbital_ref[:, start : start + CHUNK], across, preferred_element_type=jnp.float32
        )


def filter_kernel(
    counts_ref, parity_ref, plain, near_ref, far_ref, filtered_ref, first_ref, second_ref, ordered, diagonal, one, two
):
    cells, rows = plain.shape
    slots = rows // 2
    strips = BZ // SUB
    planes_y = cells // BZ
    fragments = lax.broadcasted_iota(jnp.int32, counts_ref.shape, 1)
    mine = jnp.where(fragments == lax.axis_index("dev"), counts_ref[...], 0)
    count = jnp.sum(mine, axis=1, keepdims=True)
    signed = (1.0 - 2.0 * parity_ref[...].astype(jnp.float32)) / slots
    eye = identity(CHUNK)

    for start in range(0, cells, CHUNK):
        near = jnp.broadcast_to(near_ref[0:1, start : start + CHUNK], (slots, CHUNK))
        far = jnp.broadcast_to(far_ref[0:1, start : start + CHUNK], (slots, CHUNK))
        potential = lax.dot_general(
            eye, jnp.concatenate([near, far], 0), across, preferred_element_type=jnp.float32
        )
        diagonal[start : start + CHUNK, :] = potential + (6.0 - filter_centre)

    sub_ids = lax.broadcasted_iota(jnp.int32, (SUB, rows), 0)
    is_first, is_last = sub_ids == 0, sub_ids == SUB - 1

    def strided(ref, y):
        return jnp.concatenate(
            [ref[pl.ds(y * BZ + zi, SUB, stride=strips), :] for zi in range(strips)], 0
        )

    def packed(ref, y):
        return ref[y * BZ : (y + 1) * BZ, :]

    def sweep(load, finish):
        here = load(0)
        corner = jnp.zeros((SUB, rows), jnp.float32)
        slanted_before = here
        for y in range(planes_y):
            after = load(y + 1) if y + 1 < planes_y else jnp.zeros((BZ, rows), jnp.float32)
            lower = jnp.where(is_first, 0.0, pltpu.roll(here[BZ - SUB :], 1, 0))
            slanted = after + jnp.concatenate([lower, here[: BZ - SUB]], 0)
            upper = jnp.where(is_last, corner, pltpu.roll(slanted_before[:SUB], SUB - 1, 0))
            beside = slanted + jnp.concatenate([slanted_before[SUB:], upper], 0)
            finish(y, here, beside + pltpu.roll(here, slots, 1))
            corner, slanted_before, here = here[BZ - SUB :], slanted, after

    def factor_first(y, here, beside):
        weight = strided(diagonal, y)
        ordered[y * BZ : (y + 1) * BZ, :] = weight
        one[y * BZ : (y + 1) * BZ, :] = (weight - SHIFTS[0]) * here - beside

    sweep(functools.partial(strided, plain), factor_first)

    source, target = one, two
    for shift in SHIFTS[1:-1]:

        def factor(y, here, beside, target=target, shift=shift):
            target[y * BZ : (y + 1) * BZ, :] = (packed(ordered, y) - shift) * here - beside

        sweep(functools.partial(packed, source), factor)
        source, target = target, source

    totals = [jnp.zeros((BZ, rows), jnp.float32)]

    def factor_last(y, here, beside):
        value = (packed(ordered, y) - SHIFTS[-1]) * here - beside
        for zi in range(strips):
            diagonal[pl.ds(y * BZ + zi, SUB, stride=strips), :] = value[zi * SUB : (zi + 1) * SUB]
        totals[0] = totals[0] + value * value

    sweep(functools.partial(packed, source), factor_last)

    lane_sum = jnp.broadcast_to(jnp.sum(totals[0], axis=0, keepdims=True), (SUB, rows))
    mean_square = (lane_sum + pltpu.roll(lane_sum, slots, 1)) * (LEADING * LEADING / (2 * cells))
    slot_ids = lax.broadcasted_iota(jnp.int32, (SUB, rows), 1) % slots
    scale = jnp.where(slot_ids < count, LEADING * lax.rsqrt(mean_square + 1e-06), 0.0)[:1]

    for start in range(0, cells, CHUNK):
        rounded = (diagonal[start : start + CHUNK, :] * scale).astype(jnp.bfloat16)
        turned = lax.dot_general(
            eye[:rows, :rows], rounded, across, preferred_element_type=jnp.float32
        )
        filtered_ref[:, start : start + CHUNK] = turned.astype(jnp.bfloat16)
        squares = turned * turned
        first_ref[0:1, start : start + CHUNK] = jnp.sum(squares[:slots], axis=0, keepdims=True) * signed
        second_ref[0:1, start : start + CHUNK] = jnp.sum(squares[slots:], axis=0, keepdims=True) * signed


def turn_orbitals(orbital_rows):
    rows, cells = orbital_rows.shape
    return pl.pallas_call(
        turn_kernel,
        out_shape=jax.ShapeDtypeStruct((cells, rows), jnp.float32),
        in_specs=[pl.BlockSpec(memory_space=pltpu.VMEM)],
        out_specs=pl.BlockSpec(memory_space=pltpu.VMEM),
        compiler_params=pltpu.CompilerParams(vmem_limit_bytes=8 * 2**20),
        name="turn_orbitals",
    )(orbital_rows)


def filter_box(counts, parity, plain, near, far):
    cells, rows = plain.shape
    field = pltpu.VMEM((cells, rows), jnp.float32)
    vmem = pl.BlockSpec(memory_space=pltpu.VMEM)
    half = jax.ShapeDtypeStruct((1, cells), jnp.float32)
    return pl.pallas_call(
        filter_kernel,
        out_shape=(jax.ShapeDtypeStruct((rows, cells), jnp.bfloat16), half, half),
        in_specs=[vmem] * 5,
        out_specs=(vmem, vmem, vmem),
        scratch_shapes=[field, field, field, field],
        compiler_params=pltpu.CompilerParams(vmem_limit_bytes=16 * 2**20),
        name="filter_box",
    )(counts, parity, plain, near, far)


def sum_over(part, axis):
    size = lax.axis_size(axis)
    if size & (size - 1):
        return lax.psum_scatter(part, axis, scatter_dimension=1, tiled=True)
    me = lax.axis_index(axis)
    span = size // 2
    while span:
        half = part.shape[1] // 2
        is_low = (me & span) == 0
        kept = jnp.where(is_low, part[:, :half], part[:, half:])
        sent = jnp.where(is_low, part[:, half:], part[:, :half])
        part = kept + lax.ppermute(sent, axis, [(i, i ^ span) for i in range(size)])
        span //= 2
    return part


def on_device(orbitals, potential, counts, parity):
    group_size = lax.axis_size("dev")
    slots, _, cells = orbitals.shape[2:]
    following = lax.ppermute(potential, "dev", [((i + 1) % group_size, i) for i in range(group_size)])
    orbital_rows = jnp.swapaxes(orbitals[0, 0], 0, 1).reshape(2 * slots, cells)
    plain = turn_orbitals(orbital_rows)
    filtered_rows, first, second = filter_box(counts, parity, plain, potential, following)
    carried = lax.ppermute(second, "dev", [(i, (i + 1) % group_size) for i in range(group_size)])
    density = sum_over(first + carried, "grp")
    filtered = jnp.swapaxes(filtered_rows.reshape(2, slots, cells), 0, 1)
    return density[None], filtered[None, None]


def solution(mesh):
    placed = (P("grp", "dev", None, None, None), P("dev", None), P("grp", None), P("grp", "dev"))
    return jax.shard_map(
        on_device,
        mesh=mesh,
        in_specs=placed,
        out_specs=(P("dev", None, "grp"), P("grp", "dev", None, None, None)),
        check_vma=False,
    )
```

```python
import functools
import math

import jax
import jax.numpy as jnp
from jax import lax
from jax.experimental import pallas as pl
from jax.experimental.pallas import tpu as pltpu
from jax.sharding import PartitionSpec as P

DEGREE = 8
BZ = 48
SUB = 8
CHUNK = 256

filter_centre = 9.0
filter_half = 7.0

across = (((1,), (1,)), ((), ()))


def leja_roots():
    rest = [math.cos((2 * j - 1) * math.pi / (2 * DEGREE)) for j in range(1, DEGREE + 1)]
    order = [rest.pop(0)]
    while rest:
        best = max(rest, key=lambda root: sum(math.log(abs(root - other)) for other in order))
        rest.remove(best)
        order.append(best)
    return order


SHIFTS = [filter_half * root for root in leja_roots()]
LEADING = 2.0 ** (DEGREE - 1) / filter_half**DEGREE


def identity(size):
    down = lax.broadcasted_iota(jnp.int32, (size, size), 0)
    along = lax.broadcasted_iota(jnp.int32, (size, size), 1)
    return (down == along).astype(jnp.float32).astype(jnp.bfloat16)


def eye_kernel(eye_ref):
    eye_ref[...] = identity(eye_ref.shape[0])


def turn_kernel(orbital_ref, eye_ref, plain):
    cells, rows = plain.shape
    for start in range(0, cells, CHUNK):
        part = jnp.swapaxes(orbital_ref[:, :, start : start + CHUNK], 0, 1)
        plain[start : start + CHUNK, :] = lax.dot_general(
            eye_ref[...], part.reshape(rows, CHUNK), across, preferred_element_type=jnp.float32
        )


def filter_kernel(
    counts_hbm,
    parity_any,
    plain,
    near_ref,
    far_ref,
    filtered_ref,
    halves_ref,
    counts_ref,
    parity_ref,
    ordered,
    diagonal,
    one,
    two,
    sems,
):
    cells, rows = plain.shape
    slots = rows // 2
    strips = BZ // SUB
    planes_y = cells // BZ

    small = [
        pltpu.make_async_copy(counts_hbm, counts_ref, sems.at[0]),
        pltpu.make_async_copy(parity_any, parity_ref, sems.at[1]),
    ]
    for copy in small:
        copy.start()

    eye = identity(CHUNK)
    for start in range(0, cells, CHUNK):
        near = jnp.broadcast_to(near_ref[0:1, start : start + CHUNK], (slots, CHUNK))
        far = jnp.broadcast_to(far_ref[0:1, start : start + CHUNK], (slots, CHUNK))
        potential = lax.dot_general(
            eye, jnp.concatenate([near, far], 0), across, preferred_element_type=jnp.float32
        )
        diagonal[start : start + CHUNK, :] = potential + (6.0 - filter_centre)

    sub_ids = lax.broadcasted_iota(jnp.int32, (SUB, rows), 0)
    is_first, is_last = sub_ids == 0, sub_ids == SUB - 1

    def strided(ref, y):
        return jnp.concatenate(
            [ref[pl.ds(y * BZ + zi, SUB, stride=strips), :] for zi in range(strips)], 0
        )

    def packed(ref, y):
        return ref[y * BZ : (y + 1) * BZ, :]

    def sweep(load, finish):
        here = load(0)
        corner = jnp.zeros((SUB, rows), jnp.float32)
        slanted_before = here
        for y in range(planes_y):
            after = load(y + 1) if y + 1 < planes_y else jnp.zeros((BZ, rows), jnp.float32)
            lower = jnp.where(is_first, 0.0, pltpu.roll(here[BZ - SUB :], 1, 0))
            slanted = after + jnp.concatenate([lower, here[: BZ - SUB]], 0)
            upper = jnp.where(is_last, corner, pltpu.roll(slanted_before[:SUB], SUB - 1, 0))
            beside = slanted + jnp.concatenate([slanted_before[SUB:], upper], 0)
            finish(y, here, beside + pltpu.roll(here, slots, 1))
            corner, slanted_before, here = here[BZ - SUB :], slanted, after

    def factor_first(y, here, beside):
        weight = strided(diagonal, y)
        ordered[y * BZ : (y + 1) * BZ, :] = weight
        one[y * BZ : (y + 1) * BZ, :] = (weight - SHIFTS[0]) * here - beside

    sweep(functools.partial(strided, plain), factor_first)

    source, target = one, two
    for shift in SHIFTS[1:-1]:

        def factor(y, here, beside, target=target, shift=shift):
            target[y * BZ : (y + 1) * BZ, :] = (packed(ordered, y) - shift) * here - beside

        sweep(functools.partial(packed, source), factor)
        source, target = target, source

    totals = [jnp.zeros((BZ, rows), jnp.float32)]

    def factor_last(y, here, beside):
        value = (packed(ordered, y) - SHIFTS[-1]) * here - beside
        for zi in range(strips):
            diagonal[pl.ds(y * BZ + zi, SUB, stride=strips), :] = value[zi * SUB : (zi + 1) * SUB]
        totals[0] = totals[0] + value * value

    sweep(functools.partial(packed, source), factor_last)

    for copy in small:
        copy.wait()
    count = counts_ref[0, lax.axis_index("dev")]
    signed = (1.0 - 2.0 * parity_ref[0, 0].astype(jnp.float32)) / slots

    lane_sum = jnp.broadcast_to(jnp.sum(totals[0], axis=0, keepdims=True), (SUB, rows))
    mean_square = (lane_sum + pltpu.roll(lane_sum, slots, 1)) * (LEADING * LEADING / (2 * cells))
    slot_ids = lax.broadcasted_iota(jnp.int32, (SUB, rows), 1) % slots
    scale = jnp.where(slot_ids < count, LEADING * lax.rsqrt(mean_square + 1e-06), 0.0)[:1]

    for start in range(0, cells, CHUNK):
        rounded = (diagonal[start : start + CHUNK, :] * scale).astype(jnp.bfloat16)
        turned = lax.dot_general(
            eye[:rows, :rows], rounded, across, preferred_element_type=jnp.float32
        )
        filtered_ref[:, start : start + CHUNK] = turned.astype(jnp.bfloat16)
        squares = turned * turned
        first = jnp.sum(squares[:slots], axis=0, keepdims=True)
        second = jnp.sum(squares[slots:], axis=0, keepdims=True)
        halves_ref[0:1, start : start + CHUNK] = first * signed
        halves_ref[1:2, start : start + CHUNK] = second * signed


def make_eye():
    return pl.pallas_call(
        eye_kernel,
        out_shape=jax.ShapeDtypeStruct((CHUNK, CHUNK), jnp.bfloat16),
        out_specs=pl.BlockSpec(memory_space=pltpu.VMEM),
        compiler_params=pltpu.CompilerParams(vmem_limit_bytes=2**20),
        cost_estimate=pl.CostEstimate(flops=10**10, bytes_accessed=0, transcendentals=0),
        name="make_eye",
    )()


def turn_orbitals(orbitals, eye):
    slots, planes, cells = orbitals.shape
    vmem = pl.BlockSpec(memory_space=pltpu.VMEM)
    return pl.pallas_call(
        turn_kernel,
        out_shape=jax.ShapeDtypeStruct((cells, planes * slots), jnp.float32),
        in_specs=[vmem, vmem],
        out_specs=vmem,
        compiler_params=pltpu.CompilerParams(vmem_limit_bytes=8 * 2**20),
        name="turn_orbitals",
    )(orbitals, eye)


def filter_box(counts, parity, plain, near, far):
    cells, rows = plain.shape
    field = pltpu.VMEM((cells, rows), jnp.float32)
    vmem, hbm = pl.BlockSpec(memory_space=pltpu.VMEM), pl.BlockSpec(memory_space=pltpu.HBM)
    counts = pltpu.with_memory_space_constraint(counts, pltpu.HBM)
    return pl.pallas_call(
        filter_kernel,
        out_shape=(
            jax.ShapeDtypeStruct((rows, cells), jnp.bfloat16),
            jax.ShapeDtypeStruct((2, cells), jnp.float32),
        ),
        in_specs=[hbm, pl.BlockSpec(memory_space=pl.ANY)] + [vmem] * 3,
        out_specs=(vmem, vmem),
        scratch_shapes=[pltpu.SMEM(counts.shape, jnp.int32), pltpu.SMEM(parity.shape, jnp.int32)]
        + [field] * 4
        + [pltpu.SemaphoreType.DMA((2,))],
        compiler_params=pltpu.CompilerParams(vmem_limit_bytes=16 * 2**20),
        name="filter_box",
    )(counts, parity, plain, near, far)


def sum_over(part, axis):
    size = lax.axis_size(axis)
    if size & (size - 1):
        return lax.psum_scatter(part, axis, scatter_dimension=1, tiled=True)
    me = lax.axis_index(axis)
    span = size // 2
    while span:
        half = part.shape[1] // 2
        is_low = (me & span) == 0
        kept = jnp.where(is_low, part[:, :half], part[:, half:])
        sent = jnp.where(is_low, part[:, half:], part[:, :half])
        part = kept + lax.ppermute(sent, axis, [(i, i ^ span) for i in range(size)])
        span //= 2
    return part


def on_device(orbitals, potential, counts, parity):
    group_size = lax.axis_size("dev")
    slots, _, cells = orbitals.shape[2:]
    far = lax.ppermute(potential, "dev", [((i + 1) % group_size, i) for i in range(group_size)])
    eye = make_eye()
    plain = turn_orbitals(orbitals[0, 0], eye)
    filtered_rows, halves = filter_box(counts, parity, plain, potential, far)
    halves = sum_over(halves, "grp")
    onward = [(i, (i + 1) % group_size) for i in range(group_size)]
    density = halves[:1] + lax.ppermute(halves[1:], "dev", onward)
    filtered = jnp.swapaxes(filtered_rows.reshape(2, slots, cells), 0, 1)
    return density[None], filtered[None, None]


def solution(mesh):
    placed = (P("grp", "dev", None, None, None), P("dev", None), P("grp", None), P("grp", "dev"))
    return jax.shard_map(
        on_device,
        mesh=mesh,
        in_specs=placed,
        out_specs=(P("dev", None, "grp"), P("grp", "dev", None, None, None)),
        check_vma=False,
    )
```

```python
import functools
import math

import jax
import jax.numpy as jnp
from jax import lax
from jax.experimental import pallas as pl
from jax.experimental.pallas import tpu as pltpu
from jax.sharding import PartitionSpec as P

DEGREE = 8
BZ = 48
SUB = 8
CHUNK = 128

filter_centre = 9.0
filter_half = 7.0

across = (((1,), (1,)), ((), ()))


def leja_roots():
    rest = [math.cos((2 * j - 1) * math.pi / (2 * DEGREE)) for j in range(1, DEGREE + 1)]
    order = [rest.pop(0)]
    while rest:
        best = max(rest, key=lambda root: sum(math.log(abs(root - other)) for other in order))
        rest.remove(best)
        order.append(best)
    return order


SHIFTS = [filter_half * root for root in leja_roots()]
LEADING = 2.0 ** (DEGREE - 1) / filter_half**DEGREE


def identity(size):
    down = lax.broadcasted_iota(jnp.int32, (size, size), 0)
    along = lax.broadcasted_iota(jnp.int32, (size, size), 1)
    return (down == along).astype(jnp.float32).astype(jnp.bfloat16)


def eye_kernel(eye_ref):
    eye_ref[...] = identity(eye_ref.shape[0])


def half_rows(row_ref, start, slots):
    upper = row_ref.shape[1] // 2 + start
    return [
        jnp.broadcast_to(row_ref[0:1, at : at + CHUNK], (slots, CHUNK)) for at in (start, upper)
    ]


def turn_kernel(orbital_ref, near_ref, eye_ref, plain, near_diagonal):
    slots, _, cells = orbital_ref.shape
    half, rows = cells // 2, 2 * slots
    eye = eye_ref[...]
    for start in range(0, half, CHUNK):
        lower = jnp.swapaxes(orbital_ref[:, :, start : start + CHUNK], 0, 1)
        upper = jnp.swapaxes(orbital_ref[:, :, half + start : half + start + CHUNK], 0, 1)
        parts = [lower[0], upper[0], lower[1], upper[1]] + half_rows(near_ref, start, slots)
        turned = lax.dot_general(
            eye, jnp.concatenate(parts, 0), across, preferred_element_type=jnp.float32
        )
        plain[start : start + CHUNK, :] = turned[:, :rows]
        plain[half + start : half + start + CHUNK, :] = turned[:, rows : 2 * rows]
        near_diagonal[start : start + CHUNK, :] = turned[:, 2 * rows :] + (6.0 - filter_centre)


def filter_kernel(
    counts_hbm,
    parity_any,
    plain,
    near_diagonal,
    far_ref,
    filtered_ref,
    halves_ref,
    counts_ref,
    parity_ref,
    ordered,
    far_diagonal,
    one,
    two,
    final,
    sems,
):
    cells, rows = plain.shape
    slots, half = rows // 2, cells // 2
    strips = BZ // SUB
    height = half // BZ

    small = [
        pltpu.make_async_copy(counts_hbm, counts_ref, sems.at[0]),
        pltpu.make_async_copy(parity_any, parity_ref, sems.at[1]),
    ]
    for copy in small:
        copy.start()

    eye = identity(CHUNK)
    for start in range(0, half, CHUNK):
        potential = lax.dot_general(
            eye,
            jnp.concatenate(half_rows(far_ref, start, slots), 0),
            across,
            preferred_element_type=jnp.float32,
        )
        far_diagonal[start : start + CHUNK, :] = potential + (6.0 - filter_centre)

    sub_ids = lax.broadcasted_iota(jnp.int32, (SUB, rows), 0)
    is_first, is_last = sub_ids == 0, sub_ids == SUB - 1
    is_lower = lax.broadcasted_iota(jnp.int32, (BZ, rows), 1) < slots

    def strided(ref, at):
        return jnp.concatenate(
            [ref[pl.ds(at + zi, SUB, stride=strips), :] for zi in range(strips)], 0
        )

    def packed(ref, at):
        return ref[at : at + BZ, :]

    def lowered(row):
        first = jnp.where(is_first, 0.0, pltpu.roll(row[BZ - SUB :], 1, 0))
        return jnp.concatenate([first, row[: BZ - SUB]], 0)

    def sweep(load, finish):
        here = [load(x * half) for x in range(2)]
        ends = [jnp.where(is_lower, pltpu.roll(row, slots, 1), 0.0) for row in here]
        before = [pltpu.roll(load(x * half + half - BZ), slots, 1) for x in range(2)]
        before = [jnp.where(is_lower, 0.0, row) for row in before]
        slanted = [row + lowered(last) for row, last in zip(here, before)]
        corner = [row[BZ - SUB :] for row in before]
        for y in range(height):
            after = [load(x * half + (y + 1) * BZ) if y + 1 < height else ends[x] for x in range(2)]
            for x in range(2):
                new = after[x] + lowered(here[x])
                upper = jnp.where(is_last, corner[x], pltpu.roll(slanted[x][:SUB], SUB - 1, 0))
                beside = new + jnp.concatenate([slanted[x][SUB:], upper], 0)
                finish(x, y * BZ, here[x], beside + here[1 - x])
                slanted[x] = new
            corner = [row[BZ - SUB :] for row in here]
            here = after

    def factor_first(x, at, here, beside):
        weight = strided((near_diagonal, far_diagonal)[x], at)
        at = x * half + at
        ordered[at : at + BZ, :] = weight
        one[at : at + BZ, :] = (weight - SHIFTS[0]) * here - beside

    sweep(functools.partial(strided, plain), factor_first)

    def pick(pair, shifts):
        shift = jnp.float32(shifts[0])
        for index, other in enumerate(shifts[1:], 1):
            shift = jnp.where(pair == index, jnp.float32(other), shift)
        return shift

    def factor_pair(pair, carry):
        for source, target, shifts in ((one, two, SHIFTS[1:-1:2]), (two, one, SHIFTS[2:-1:2])):
            shift = pick(pair, shifts)

            def factor(x, at, here, beside, target=target, shift=shift):
                at = x * half + at
                target[at : at + BZ, :] = (packed(ordered, at) - shift) * here - beside

            sweep(functools.partial(packed, source), factor)
        return carry

    lax.fori_loop(0, (DEGREE - 2) // 2, factor_pair, 0)

    totals = [jnp.zeros((BZ, rows), jnp.float32)]

    def factor_last(x, at, here, beside):
        at = x * half + at
        value = (packed(ordered, at) - SHIFTS[-1]) * here - beside
        for zi in range(strips):
            final[pl.ds(at + zi, SUB, stride=strips), :] = value[zi * SUB : (zi + 1) * SUB]
        totals[0] = totals[0] + value * value

    sweep(functools.partial(packed, one), factor_last)

    for copy in small:
        copy.wait()
    count = counts_ref[0, lax.axis_index("dev")]
    signed = (1.0 - 2.0 * parity_ref[0, 0].astype(jnp.float32)) / slots

    lane_sum = jnp.broadcast_to(jnp.sum(totals[0], axis=0, keepdims=True), (SUB, rows))
    mean_square = (lane_sum + pltpu.roll(lane_sum, slots, 1)) * (LEADING * LEADING / (2 * cells))
    slot_ids = lax.broadcasted_iota(jnp.int32, (SUB, rows), 1) % slots
    scale = jnp.where(slot_ids < count, LEADING * lax.rsqrt(mean_square + 1e-06), 0.0)[:1]

    wide = 3 * CHUNK if half % (3 * CHUNK) == 0 else CHUNK
    for x in range(2):
        for start in range(0, half, wide):
            at = x * half + start
            rounded = (final[at : at + wide, :] * scale).astype(jnp.bfloat16)
            turned = lax.dot_general(eye, rounded, across, preferred_element_type=jnp.float32)
            rounded = turned.astype(jnp.bfloat16)
            squares = turned * turned
            for part in range(2):
                mine = slice(part * slots, (part + 1) * slots)
                to = slice(part * half + start, part * half + start + wide)
                filtered_ref[x * slots : (x + 1) * slots, to] = rounded[mine]
                halves_ref[x : x + 1, to] = jnp.sum(squares[mine], axis=0, keepdims=True) * signed


def make_eye():
    return pl.pallas_call(
        eye_kernel,
        out_shape=jax.ShapeDtypeStruct((CHUNK, CHUNK), jnp.bfloat16),
        out_specs=pl.BlockSpec(memory_space=pltpu.VMEM),
        compiler_params=pltpu.CompilerParams(vmem_limit_bytes=2**20),
        cost_estimate=pl.CostEstimate(flops=10**10, bytes_accessed=0, transcendentals=0),
        name="make_eye",
    )()


def turn_orbitals(orbitals, near, eye):
    slots, planes, cells = orbitals.shape
    vmem = pl.BlockSpec(memory_space=pltpu.VMEM)
    return pl.pallas_call(
        turn_kernel,
        out_shape=(
            jax.ShapeDtypeStruct((cells, planes * slots), jnp.float32),
            jax.ShapeDtypeStruct((cells // 2, planes * slots), jnp.float32),
        ),
        in_specs=[vmem] * 3,
        out_specs=(vmem, vmem),
        compiler_params=pltpu.CompilerParams(vmem_limit_bytes=8 * 2**20),
        name="turn_orbitals",
    )(orbitals, near, eye)


def filter_box(counts, parity, plain, near_diagonal, far):
    cells, rows = plain.shape
    field, half = pltpu.VMEM((cells, rows), jnp.float32), pltpu.VMEM((cells // 2, rows), jnp.float32)
    vmem, hbm = pl.BlockSpec(memory_space=pltpu.VMEM), pl.BlockSpec(memory_space=pltpu.HBM)
    counts = pltpu.with_memory_space_constraint(counts, pltpu.HBM)
    return pl.pallas_call(
        filter_kernel,
        out_shape=(
            jax.ShapeDtypeStruct((rows, cells), jnp.bfloat16),
            jax.ShapeDtypeStruct((2, cells), jnp.float32),
        ),
        in_specs=[hbm, pl.BlockSpec(memory_space=pl.ANY)] + [vmem] * 3,
        out_specs=(vmem, vmem),
        scratch_shapes=[pltpu.SMEM(counts.shape, jnp.int32), pltpu.SMEM(parity.shape, jnp.int32)]
        + [field, half, field, field, field]
        + [pltpu.SemaphoreType.DMA((2,))],
        compiler_params=pltpu.CompilerParams(vmem_limit_bytes=16 * 2**20),
        name="filter_box",
    )(counts, parity, plain, near_diagonal, far)


def sum_over(part, axis):
    size = lax.axis_size(axis)
    if size & (size - 1):
        return lax.psum_scatter(part, axis, scatter_dimension=1, tiled=True)
    me = lax.axis_index(axis)
    span = size // 2
    while span:
        half = part.shape[1] // 2
        is_low = (me & span) == 0
        kept = jnp.where(is_low, part[:, :half], part[:, half:])
        sent = jnp.where(is_low, part[:, half:], part[:, :half])
        part = kept + lax.ppermute(sent, axis, [(i, i ^ span) for i in range(size)])
        span //= 2
    return part


def on_device(orbitals, potential, counts, parity):
    group_size = lax.axis_size("dev")
    slots, _, cells = orbitals.shape[2:]
    far = lax.ppermute(potential, "dev", [((i + 1) % group_size, i) for i in range(group_size)])
    eye = make_eye()
    plain, near_diagonal = turn_orbitals(orbitals[0, 0], potential, eye)
    filtered_rows, halves = filter_box(counts, parity, plain, near_diagonal, far)
    halves = sum_over(halves, "grp")
    onward = [(i, (i + 1) % group_size) for i in range(group_size)]
    density = halves[:1] + lax.ppermute(halves[1:], "dev", onward)
    filtered = jnp.swapaxes(filtered_rows.reshape(2, slots, cells), 0, 1)
    return density[None], filtered[None, None]


def solution(mesh):
    placed = (P("grp", "dev", None, None, None), P("dev", None), P("grp", None), P("grp", "dev"))
    return jax.shard_map(
        on_device,
        mesh=mesh,
        in_specs=placed,
        out_specs=(P("dev", None, "grp"), P("grp", "dev", None, None, None)),
        check_vma=False,
    )
```

```python
import functools
import math

import jax
import jax.numpy as jnp
from jax import lax
from jax.experimental import pallas as pl
from jax.experimental.pallas import tpu as pltpu
from jax.sharding import PartitionSpec as P

DEGREE = 8
BZ = 48
SUB = 8
CHUNK = 128

filter_centre = 9.0
filter_half = 7.0

across = (((1,), (1,)), ((), ()))


def leja_roots():
    rest = [math.cos((2 * j - 1) * math.pi / (2 * DEGREE)) for j in range(1, DEGREE + 1)]
    order = [rest.pop(0)]
    while rest:
        best = max(rest, key=lambda root: sum(math.log(abs(root - other)) for other in order))
        rest.remove(best)
        order.append(best)
    return order


SHIFTS = [filter_half * root + filter_centre - 6.0 for root in leja_roots()]
LEADING = 2.0 ** (DEGREE - 1) / filter_half**DEGREE


def identity(size):
    down = lax.broadcasted_iota(jnp.int32, (size, size), 0)
    along = lax.broadcasted_iota(jnp.int32, (size, size), 1)
    return (down == along).astype(jnp.float32).astype(jnp.bfloat16)


def eye_kernel(eye_ref):
    eye_ref[...] = identity(eye_ref.shape[0])


def half_rows(row_ref, start, slots):
    upper = row_ref.shape[1] // 2 + start
    return [
        jnp.broadcast_to(row_ref[0:1, at : at + CHUNK], (slots, CHUNK)) for at in (start, upper)
    ]


def turn_kernel(orbital_ref, near_ref, eye_ref, plain, near_diagonal):
    slots, _, cells = orbital_ref.shape
    half, rows = cells // 2, 2 * slots
    eye = eye_ref[...]
    for start in range(0, half, CHUNK):
        lower = jnp.swapaxes(orbital_ref[:, :, start : start + CHUNK], 0, 1)
        upper = jnp.swapaxes(orbital_ref[:, :, half + start : half + start + CHUNK], 0, 1)
        parts = [lower[0], upper[0], lower[1], upper[1]] + half_rows(near_ref, start, slots)
        turned = lax.dot_general(
            eye, jnp.concatenate(parts, 0), across, preferred_element_type=jnp.float32
        )
        plain[start : start + CHUNK, :] = turned[:, :rows]
        plain[half + start : half + start + CHUNK, :] = turned[:, rows : 2 * rows]
        near_diagonal[start : start + CHUNK, :] = turned[:, 2 * rows :]


def filter_kernel(
    marks_ref,
    plain,
    near_diagonal,
    far_ref,
    filtered_ref,
    halves_ref,
    ordered,
    far_diagonal,
    one,
    two,
    final,
):
    cells, rows = plain.shape
    slots, half = rows // 2, cells // 2
    strips = BZ // SUB
    height = half // BZ

    eye = identity(CHUNK)
    for start in range(0, half, CHUNK):
        potential = lax.dot_general(
            eye,
            jnp.concatenate(half_rows(far_ref, start, slots), 0),
            across,
            preferred_element_type=jnp.float32,
        )
        far_diagonal[start : start + CHUNK, :] = potential

    sub_ids = lax.broadcasted_iota(jnp.int32, (SUB, rows), 0)
    is_first, is_last = sub_ids == 0, sub_ids == SUB - 1
    is_lower = lax.broadcasted_iota(jnp.int32, (BZ, rows), 1) < slots

    def strided(ref, at):
        return jnp.concatenate(
            [ref[pl.ds(at + zi, SUB, stride=strips), :] for zi in range(strips)], 0
        )

    def packed(ref, at):
        return ref[at : at + BZ, :]

    def lowered(row):
        first = jnp.where(is_first, 0.0, pltpu.roll(row[BZ - SUB :], 1, 0))
        return jnp.concatenate([first, row[: BZ - SUB]], 0)

    def sweep(load, finish):
        here = [load(x * half) for x in range(2)]
        ends = [jnp.where(is_lower, pltpu.roll(row, slots, 1), 0.0) for row in here]
        before = [pltpu.roll(load(x * half + half - BZ), slots, 1) for x in range(2)]
        before = [jnp.where(is_lower, 0.0, row) for row in before]
        slanted = [row + lowered(last) for row, last in zip(here, before)]
        corner = [row[BZ - SUB :] for row in before]
        for y in range(height):
            after = [load(x * half + (y + 1) * BZ) if y + 1 < height else ends[x] for x in range(2)]
            for x in range(2):
                new = after[x] + lowered(here[x])
                upper = jnp.where(is_last, corner[x], pltpu.roll(slanted[x][:SUB], SUB - 1, 0))
                beside = new + jnp.concatenate([slanted[x][SUB:], upper], 0)
                finish(x, y * BZ, here[x], beside + here[1 - x])
                slanted[x] = new
            corner = [row[BZ - SUB :] for row in here]
            here = after

    def factor_first(x, at, here, beside):
        weight = strided((near_diagonal, far_diagonal)[x], at)
        at = x * half + at
        ordered[at : at + BZ, :] = weight
        one[at : at + BZ, :] = (weight - SHIFTS[0]) * here - beside

    sweep(functools.partial(strided, plain), factor_first)

    def pick(pair, shifts):
        shift = jnp.float32(shifts[0])
        for index, other in enumerate(shifts[1:], 1):
            shift = jnp.where(pair == index, jnp.float32(other), shift)
        return shift

    def factor_pair(pair, carry):
        for source, target, shifts in ((one, two, SHIFTS[1:-1:2]), (two, one, SHIFTS[2:-1:2])):
            shift = pick(pair, shifts)

            def factor(x, at, here, beside, target=target, shift=shift):
                at = x * half + at
                target[at : at + BZ, :] = (packed(ordered, at) - shift) * here - beside

            sweep(functools.partial(packed, source), factor)
        return carry

    lax.fori_loop(0, (DEGREE - 2) // 2, factor_pair, 0)

    totals = [jnp.zeros((BZ, rows), jnp.float32)]

    def factor_last(x, at, here, beside):
        at = x * half + at
        value = (packed(ordered, at) - SHIFTS[-1]) * here - beside
        for zi in range(strips):
            final[pl.ds(at + zi, SUB, stride=strips), :] = value[zi * SUB : (zi + 1) * SUB]
        totals[0] = totals[0] + value * value

    sweep(functools.partial(packed, one), factor_last)

    marks = marks_ref[...]
    places = lax.broadcasted_iota(jnp.int32, marks.shape, 1)
    count = jnp.sum(jnp.where(places == lax.axis_index("dev"), marks, 0), axis=1, keepdims=True)
    parity = jnp.sum(jnp.where(places == marks.shape[1] - 1, marks, 0), axis=1, keepdims=True)
    signed = (1.0 - 2.0 * parity.astype(jnp.float32)) / slots

    lane_sum = jnp.broadcast_to(jnp.sum(totals[0], axis=0, keepdims=True), (SUB, rows))
    mean_square = (lane_sum + pltpu.roll(lane_sum, slots, 1)) * (LEADING * LEADING / (2 * cells))
    slot_ids = lax.broadcasted_iota(jnp.int32, (SUB, rows), 1) % slots
    scale = jnp.where(slot_ids < count, LEADING * lax.rsqrt(mean_square + 1e-06), 0.0)[:1]

    wide = 9 * CHUNK
    for x in range(2):
        for start in range(0, half, wide):
            at = x * half + start
            rounded = (final[at : at + wide, :] * scale).astype(jnp.bfloat16)
            turned = lax.dot_general(eye, rounded, across, preferred_element_type=jnp.float32)
            rounded = turned.astype(jnp.bfloat16)
            squares = turned * turned
            for part in range(2):
                mine = slice(part * slots, (part + 1) * slots)
                to = slice(part * half + start, part * half + start + wide)
                filtered_ref[x * slots : (x + 1) * slots, to] = rounded[mine]
                halves_ref[x : x + 1, to] = jnp.sum(squares[mine], axis=0, keepdims=True) * signed


def make_eye():
    return pl.pallas_call(
        eye_kernel,
        out_shape=jax.ShapeDtypeStruct((CHUNK, CHUNK), jnp.bfloat16),
        out_specs=pl.BlockSpec(memory_space=pltpu.VMEM),
        compiler_params=pltpu.CompilerParams(vmem_limit_bytes=2**20),
        cost_estimate=pl.CostEstimate(flops=10**10, bytes_accessed=0, transcendentals=0),
        name="make_eye",
    )()


def turn_orbitals(orbitals, near, eye):
    slots, planes, cells = orbitals.shape
    vmem = pl.BlockSpec(memory_space=pltpu.VMEM)
    return pl.pallas_call(
        turn_kernel,
        out_shape=(
            jax.ShapeDtypeStruct((cells, planes * slots), jnp.float32),
            jax.ShapeDtypeStruct((cells // 2, planes * slots), jnp.float32),
        ),
        in_specs=[vmem] * 3,
        out_specs=(vmem, vmem),
        compiler_params=pltpu.CompilerParams(vmem_limit_bytes=8 * 2**20),
        name="turn_orbitals",
    )(orbitals, near, eye)


def filter_box(marks, plain, near_diagonal, far):
    cells, rows = plain.shape
    field, half = pltpu.VMEM((cells, rows), jnp.float32), pltpu.VMEM((cells // 2, rows), jnp.float32)
    vmem = pl.BlockSpec(memory_space=pltpu.VMEM)
    return pl.pallas_call(
        filter_kernel,
        out_shape=(
            jax.ShapeDtypeStruct((rows, cells), jnp.bfloat16),
            jax.ShapeDtypeStruct((2, cells), jnp.float32),
        ),
        in_specs=[vmem] * 4,
        out_specs=(vmem, vmem),
        scratch_shapes=[field, half, field, field, field],
        compiler_params=pltpu.CompilerParams(vmem_limit_bytes=16 * 2**20),
        name="filter_box",
    )(marks, plain, near_diagonal, far)


def by_halves(part, span):
    half = part.shape[1] // 2
    is_low = (lax.axis_index("grp") & span) == 0
    low, high = part[:, :half], part[:, half:]
    return jnp.where(is_low, low, high), jnp.where(is_low, high, low)


def sum_blocks(halves):
    groups, devs = lax.axis_size("grp"), lax.axis_size("dev")
    onward = [(d, (d + 1) % devs) for d in range(devs)]
    if groups & (groups - 1) or groups == 1:
        sums = lax.psum_scatter(halves, "grp", scatter_dimension=1, tiled=True)
        return sums[:1] + lax.ppermute(sums[1:], "dev", onward)
    span = groups // 2
    while span > 1:
        mine, other = by_halves(halves, span)
        halves = mine + lax.ppermute(other, "grp", [(g, g ^ span) for g in range(groups)])
        span //= 2
    mine, other = by_halves(halves, 1)
    both_axes = ("grp", "dev")
    places = [(g, d) for g in range(groups) for d in range(devs)]
    carried = lax.ppermute(mine[1:], both_axes, [(g * devs + d, g * devs + (d + 1) % devs) for g, d in places])
    beside = lax.ppermute(other[:1], both_axes, [(g * devs + d, (g ^ 1) * devs + d) for g, d in places])
    slanted = lax.ppermute(other[1:], both_axes, [(g * devs + d, (g ^ 1) * devs + (d + 1) % devs) for g, d in places])
    return mine[:1] + carried + beside + slanted


def on_device(orbitals, potential, counts, parity):
    group_size = lax.axis_size("dev")
    slots, _, cells = orbitals.shape[2:]
    far = lax.ppermute(potential, "dev", [((i + 1) % group_size, i) for i in range(group_size)])
    marks = jnp.concatenate([counts, parity], 1)
    eye = make_eye()
    plain, near_diagonal = turn_orbitals(orbitals[0, 0], potential, eye)
    filtered_rows, halves = filter_box(marks, plain, near_diagonal, far)
    density = sum_blocks(halves)
    filtered = jnp.swapaxes(filtered_rows.reshape(2, slots, cells), 0, 1)
    return density[None], filtered[None, None]


def solution(mesh):
    placed = (P("grp", "dev", None, None, None), P("dev", None), P("grp", None), P("grp", "dev"))
    return jax.shard_map(
        on_device,
        mesh=mesh,
        in_specs=placed,
        out_specs=(P("dev", None, "grp"), P("grp", "dev", None, None, None)),
        check_vma=False,
    )
```

```python
import functools
import math

import jax
import jax.numpy as jnp
from jax import lax
from jax.experimental import pallas as pl
from jax.experimental.pallas import tpu as pltpu
from jax.sharding import PartitionSpec as P

DEGREE = 8
BZ = 48
SUB = 8
CHUNK = 128

filter_centre = 9.0
filter_half = 7.0

across = (((1,), (1,)), ((), ()))


def leja_roots():
    rest = [math.cos((2 * j - 1) * math.pi / (2 * DEGREE)) for j in range(1, DEGREE + 1)]
    order = [rest.pop(0)]
    while rest:
        best = max(rest, key=lambda root: sum(math.log(abs(root - other)) for other in order))
        rest.remove(best)
        order.append(best)
    return order


SHIFTS = [filter_half * root + filter_centre - 6.0 for root in leja_roots()]
LEADING = 2.0 ** (DEGREE - 1) / filter_half**DEGREE


def identity(size):
    down = lax.broadcasted_iota(jnp.int32, (size, size), 0)
    along = lax.broadcasted_iota(jnp.int32, (size, size), 1)
    return (down == along).astype(jnp.float32).astype(jnp.bfloat16)


def eye_kernel(eye_ref):
    eye_ref[...] = identity(eye_ref.shape[0])


def half_rows(row_ref, start, slots):
    upper = row_ref.shape[1] // 2 + start
    return [
        jnp.broadcast_to(row_ref[0:1, at : at + CHUNK], (slots, CHUNK)) for at in (start, upper)
    ]


def turn_kernel(orbital_ref, near_ref, eye_ref, plain, near_diagonal):
    slots, _, cells = orbital_ref.shape
    half, rows = cells // 2, 2 * slots
    eye = eye_ref[...]
    for start in range(0, half, CHUNK):
        lower = jnp.swapaxes(orbital_ref[:, :, start : start + CHUNK], 0, 1)
        upper = jnp.swapaxes(orbital_ref[:, :, half + start : half + start + CHUNK], 0, 1)
        parts = [lower[0], upper[0], lower[1], upper[1]] + half_rows(near_ref, start, slots)
        turned = lax.dot_general(
            eye, jnp.concatenate(parts, 0), across, preferred_element_type=jnp.float32
        )
        plain[start : start + CHUNK, :] = turned[:, :rows]
        plain[half + start : half + start + CHUNK, :] = turned[:, rows : 2 * rows]
        near_diagonal[start : start + CHUNK, :] = turned[:, 2 * rows :]


def filter_kernel(
    marks_ref,
    plain,
    near_diagonal,
    far_ref,
    filtered_ref,
    halves_ref,
    ordered,
    far_diagonal,
    one,
    two,
    final,
):
    cells, rows = plain.shape
    slots, half = rows // 2, cells // 2
    strips = BZ // SUB
    height = half // BZ

    eye = identity(CHUNK)
    for start in range(0, half, CHUNK):
        potential = lax.dot_general(
            eye,
            jnp.concatenate(half_rows(far_ref, start, slots), 0),
            across,
            preferred_element_type=jnp.float32,
        )
        far_diagonal[start : start + CHUNK, :] = potential

    sub_ids = lax.broadcasted_iota(jnp.int32, (SUB, rows), 0)
    is_first, is_last = sub_ids == 0, sub_ids == SUB - 1
    is_lower = lax.broadcasted_iota(jnp.int32, (BZ, rows), 1) < slots

    def strided(ref, at):
        return jnp.concatenate(
            [ref[pl.ds(at + zi, SUB, stride=strips), :] for zi in range(strips)], 0
        )

    def packed(ref, at):
        return ref[at : at + BZ, :]

    def lowered(row):
        first = jnp.where(is_first, 0.0, pltpu.roll(row[BZ - SUB :], 1, 0))
        return jnp.concatenate([first, row[: BZ - SUB]], 0)

    def sweep(load, finish):
        here = [load(x * half) for x in range(2)]
        ends = [jnp.where(is_lower, pltpu.roll(row, slots, 1), 0.0) for row in here]
        before = [pltpu.roll(load(x * half + half - BZ), slots, 1) for x in range(2)]
        before = [jnp.where(is_lower, 0.0, row) for row in before]
        slanted = [row + lowered(last) for row, last in zip(here, before)]
        corner = [row[BZ - SUB :] for row in before]
        for y in range(height):
            after = [load(x * half + (y + 1) * BZ) if y + 1 < height else ends[x] for x in range(2)]
            for x in range(2):
                new = after[x] + lowered(here[x])
                upper = jnp.where(is_last, corner[x], pltpu.roll(slanted[x][:SUB], SUB - 1, 0))
                beside = new + jnp.concatenate([slanted[x][SUB:], upper], 0)
                finish(x, y * BZ, here[x], beside + here[1 - x])
                slanted[x] = new
            corner = [row[BZ - SUB :] for row in here]
            here = after

    def factor_first(x, at, here, beside):
        weight = strided((near_diagonal, far_diagonal)[x], at)
        at = x * half + at
        ordered[at : at + BZ, :] = weight
        one[at : at + BZ, :] = (weight - SHIFTS[0]) * here - beside

    sweep(functools.partial(strided, plain), factor_first)

    def pick(pair, shifts):
        shift = jnp.float32(shifts[0])
        for index, other in enumerate(shifts[1:], 1):
            shift = jnp.where(pair == index, jnp.float32(other), shift)
        return shift

    def factor_pair(pair, carry):
        for source, target, shifts in ((one, two, SHIFTS[1:-1:2]), (two, one, SHIFTS[2:-1:2])):
            shift = pick(pair, shifts)

            def factor(x, at, here, beside, target=target, shift=shift):
                at = x * half + at
                target[at : at + BZ, :] = (packed(ordered, at) - shift) * here - beside

            sweep(functools.partial(packed, source), factor)
        return carry

    lax.fori_loop(0, (DEGREE - 2) // 2, factor_pair, 0)

    totals = [jnp.zeros((BZ, rows), jnp.float32)]

    def factor_last(x, at, here, beside):
        at = x * half + at
        value = (packed(ordered, at) - SHIFTS[-1]) * here - beside
        for zi in range(strips):
            final[pl.ds(at + zi, SUB, stride=strips), :] = value[zi * SUB : (zi + 1) * SUB]
        totals[0] = totals[0] + value * value

    sweep(functools.partial(packed, one), factor_last)

    marks = marks_ref[...]
    places = lax.broadcasted_iota(jnp.int32, marks.shape, 1)
    count = jnp.sum(jnp.where(places == lax.axis_index("dev"), marks, 0), axis=1, keepdims=True)
    parity = jnp.sum(jnp.where(places == marks.shape[1] - 1, marks, 0), axis=1, keepdims=True)
    signed = (1.0 - 2.0 * parity.astype(jnp.float32)) / slots

    lane_sum = jnp.broadcast_to(jnp.sum(totals[0], axis=0, keepdims=True), (SUB, rows))
    mean_square = (lane_sum + pltpu.roll(lane_sum, slots, 1)) * (LEADING * LEADING / (2 * cells))
    slot_ids = lax.broadcasted_iota(jnp.int32, (SUB, rows), 1) % slots
    scale = jnp.where(slot_ids < count, LEADING * lax.rsqrt(mean_square + 1e-06), 0.0)[:1]

    wide = 9 * CHUNK
    for x in range(2):
        for start in range(0, half, wide):
            at = x * half + start
            rounded = (final[at : at + wide, :] * scale).astype(jnp.bfloat16)
            turned = lax.dot_general(eye, rounded, across, preferred_element_type=jnp.float32)
            rounded = turned.astype(jnp.bfloat16)
            squares = turned * turned
            for part in range(2):
                mine = slice(part * slots, (part + 1) * slots)
                to = slice(part * half + start, part * half + start + wide)
                filtered_ref[x * slots : (x + 1) * slots, to] = rounded[mine]
                halves_ref[x : x + 1, to] = jnp.sum(squares[mine], axis=0, keepdims=True) * signed


def make_eye():
    return pl.pallas_call(
        eye_kernel,
        out_shape=jax.ShapeDtypeStruct((CHUNK, CHUNK), jnp.bfloat16),
        out_specs=pl.BlockSpec(memory_space=pltpu.VMEM),
        compiler_params=pltpu.CompilerParams(vmem_limit_bytes=2**20),
        cost_estimate=pl.CostEstimate(flops=10**10, bytes_accessed=0, transcendentals=0),
        name="make_eye",
    )()


def turn_orbitals(orbitals, near, eye):
    slots, planes, cells = orbitals.shape
    vmem = pl.BlockSpec(memory_space=pltpu.VMEM)
    return pl.pallas_call(
        turn_kernel,
        out_shape=(
            jax.ShapeDtypeStruct((cells, planes * slots), jnp.float32),
            jax.ShapeDtypeStruct((cells // 2, planes * slots), jnp.float32),
        ),
        in_specs=[vmem] * 3,
        out_specs=(vmem, vmem),
        compiler_params=pltpu.CompilerParams(vmem_limit_bytes=8 * 2**20),
        name="turn_orbitals",
    )(orbitals, near, eye)


def filter_box(marks, plain, near_diagonal, far):
    cells, rows = plain.shape
    field, half = pltpu.VMEM((cells, rows), jnp.float32), pltpu.VMEM((cells // 2, rows), jnp.float32)
    vmem = pl.BlockSpec(memory_space=pltpu.VMEM)
    return pl.pallas_call(
        filter_kernel,
        out_shape=(
            jax.ShapeDtypeStruct((rows, cells), jnp.bfloat16),
            jax.ShapeDtypeStruct((2, cells), jnp.float32),
        ),
        in_specs=[vmem] * 4,
        out_specs=(vmem, vmem),
        scratch_shapes=[field, half, field, field, field],
        compiler_params=pltpu.CompilerParams(vmem_limit_bytes=16 * 2**20),
        name="filter_box",
    )(marks, plain, near_diagonal, far)


def by_halves(part, span):
    half = part.shape[1] // 2
    is_low = (lax.axis_index("grp") & span) == 0
    low, high = part[:, :half], part[:, half:]
    return jnp.where(is_low, low, high), jnp.where(is_low, high, low)


def sum_blocks(halves):
    groups, devs = lax.axis_size("grp"), lax.axis_size("dev")
    onward = [(d, (d + 1) % devs) for d in range(devs)]
    if groups & (groups - 1) or groups == 1:
        sums = lax.psum_scatter(halves, "grp", scatter_dimension=1, tiled=True)
        return sums[:1] + lax.ppermute(sums[1:], "dev", onward)
    span = groups // 2
    while span > 1:
        mine, other = by_halves(halves, span)
        halves = mine + lax.ppermute(other, "grp", [(g, g ^ span) for g in range(groups)])
        span //= 2
    mine, other = by_halves(halves, 1)
    both_axes = ("grp", "dev")
    places = [(g, d) for g in range(groups) for d in range(devs)]
    carried = lax.ppermute(mine[1:], both_axes, [(g * devs + d, g * devs + (d + 1) % devs) for g, d in places])
    beside = lax.ppermute(other[:1], both_axes, [(g * devs + d, (g ^ 1) * devs + d) for g, d in places])
    slanted = lax.ppermute(other[1:], both_axes, [(g * devs + d, (g ^ 1) * devs + (d + 1) % devs) for g, d in places])
    return mine[:1] + carried + slanted + beside


def on_device(orbitals, potential, counts, parity):
    group_size = lax.axis_size("dev")
    slots, _, cells = orbitals.shape[2:]
    far = lax.ppermute(potential, "dev", [((i + 1) % group_size, i) for i in range(group_size)])
    marks = jnp.concatenate([counts, parity], 1)
    eye = make_eye()
    plain, near_diagonal = turn_orbitals(orbitals[0, 0], potential, eye)
    filtered_rows, halves = filter_box(marks, plain, near_diagonal, far)
    density = sum_blocks(halves)
    filtered = jnp.swapaxes(filtered_rows.reshape(2, slots, cells), 0, 1)
    return density[None], filtered[None, None]


def solution(mesh):
    placed = (P("grp", "dev", None, None, None), P("dev", None), P("grp", None), P("grp", "dev"))
    return jax.shard_map(
        on_device,
        mesh=mesh,
        in_specs=placed,
        out_specs=(P("dev", None, "grp"), P("grp", "dev", None, None, None)),
        check_vma=False,
    )
```

```python
import functools
import math

import jax
import jax.numpy as jnp
from jax import lax
from jax.experimental import pallas as pl
from jax.experimental.pallas import tpu as pltpu
from jax.sharding import PartitionSpec as P

DEGREE = 8
BZ = 48
SUB = 8
CHUNK = 128

filter_centre = 9.0
filter_half = 7.0

across = (((1,), (1,)), ((), ()))


def leja_roots():
    rest = [math.cos((2 * j - 1) * math.pi / (2 * DEGREE)) for j in range(1, DEGREE + 1)]
    order = [rest.pop(0)]
    while rest:
        best = max(rest, key=lambda root: sum(math.log(abs(root - other)) for other in order))
        rest.remove(best)
        order.append(best)
    return order


SHIFTS = [filter_half * root + filter_centre - 6.0 for root in leja_roots()]
LEADING = 2.0 ** (DEGREE - 1) / filter_half**DEGREE


def identity(size):
    down = lax.broadcasted_iota(jnp.int32, (size, size), 0)
    along = lax.broadcasted_iota(jnp.int32, (size, size), 1)
    return (down == along).astype(jnp.float32).astype(jnp.bfloat16)


def eye_kernel(eye_ref):
    eye_ref[...] = identity(eye_ref.shape[0])


def half_rows(row_ref, start, slots):
    upper = row_ref.shape[1] // 2 + start
    return [
        jnp.broadcast_to(row_ref[0:1, at : at + CHUNK], (slots, CHUNK)) for at in (start, upper)
    ]


def turn_kernel(orbital_ref, near_ref, eye_ref, plain, near_diagonal):
    slots, _, cells = orbital_ref.shape
    half, rows = cells // 2, 2 * slots
    eye = eye_ref[...]
    for start in range(0, half, CHUNK):
        lower = jnp.swapaxes(orbital_ref[:, :, start : start + CHUNK], 0, 1)
        upper = jnp.swapaxes(orbital_ref[:, :, half + start : half + start + CHUNK], 0, 1)
        parts = [lower[0], upper[0], lower[1], upper[1]] + half_rows(near_ref, start, slots)
        turned = lax.dot_general(
            eye, jnp.concatenate(parts, 0), across, preferred_element_type=jnp.float32
        )
        plain[start : start + CHUNK, :] = turned[:, :rows]
        plain[half + start : half + start + CHUNK, :] = turned[:, rows : 2 * rows]
        near_diagonal[start : start + CHUNK, :] = turned[:, 2 * rows :]


def filter_kernel(
    marks_ref,
    plain,
    near_diagonal,
    far_ref,
    filtered_ref,
    kept_ref,
    sent_ref,
    halves_ref,
    ordered,
    far_diagonal,
    one,
    two,
    final,
):
    cells, rows = plain.shape
    slots, half = rows // 2, cells // 2
    strips = BZ // SUB
    height = half // BZ

    eye = identity(CHUNK)
    for start in range(0, half, CHUNK):
        potential = lax.dot_general(
            eye,
            jnp.concatenate(half_rows(far_ref, start, slots), 0),
            across,
            preferred_element_type=jnp.float32,
        )
        far_diagonal[start : start + CHUNK, :] = potential

    sub_ids = lax.broadcasted_iota(jnp.int32, (SUB, rows), 0)
    is_first, is_last = sub_ids == 0, sub_ids == SUB - 1
    is_lower = lax.broadcasted_iota(jnp.int32, (BZ, rows), 1) < slots

    def strided(ref, at):
        return jnp.concatenate(
            [ref[pl.ds(at + zi, SUB, stride=strips), :] for zi in range(strips)], 0
        )

    def packed(ref, at):
        return ref[at : at + BZ, :]

    def lowered(row):
        first = jnp.where(is_first, 0.0, pltpu.roll(row[BZ - SUB :], 1, 0))
        return jnp.concatenate([first, row[: BZ - SUB]], 0)

    def sweep(load, finish):
        here = [load(x * half) for x in range(2)]
        ends = [jnp.where(is_lower, pltpu.roll(row, slots, 1), 0.0) for row in here]
        before = [pltpu.roll(load(x * half + half - BZ), slots, 1) for x in range(2)]
        before = [jnp.where(is_lower, 0.0, row) for row in before]
        slanted = [row + lowered(last) for row, last in zip(here, before)]
        corner = [row[BZ - SUB :] for row in before]
        for y in range(height):
            after = [load(x * half + (y + 1) * BZ) if y + 1 < height else ends[x] for x in range(2)]
            for x in range(2):
                new = after[x] + lowered(here[x])
                upper = jnp.where(is_last, corner[x], pltpu.roll(slanted[x][:SUB], SUB - 1, 0))
                beside = new + jnp.concatenate([slanted[x][SUB:], upper], 0)
                finish(x, y * BZ, here[x], beside + here[1 - x])
                slanted[x] = new
            corner = [row[BZ - SUB :] for row in here]
            here = after

    def factor_first(x, at, here, beside):
        weight = strided((near_diagonal, far_diagonal)[x], at)
        at = x * half + at
        ordered[at : at + BZ, :] = weight
        one[at : at + BZ, :] = (weight - SHIFTS[0]) * here - beside

    sweep(functools.partial(strided, plain), factor_first)

    def pick(pair, shifts):
        shift = jnp.float32(shifts[0])
        for index, other in enumerate(shifts[1:], 1):
            shift = jnp.where(pair == index, jnp.float32(other), shift)
        return shift

    def factor_pair(pair, carry):
        for source, target, shifts in ((one, two, SHIFTS[1:-1:2]), (two, one, SHIFTS[2:-1:2])):
            shift = pick(pair, shifts)

            def factor(x, at, here, beside, target=target, shift=shift):
                at = x * half + at
                target[at : at + BZ, :] = (packed(ordered, at) - shift) * here - beside

            sweep(functools.partial(packed, source), factor)
        return carry

    lax.fori_loop(0, (DEGREE - 2) // 2, factor_pair, 0)

    totals = [jnp.zeros((BZ, rows), jnp.float32)]

    def factor_last(x, at, here, beside):
        at = x * half + at
        value = (packed(ordered, at) - SHIFTS[-1]) * here - beside
        for zi in range(strips):
            final[pl.ds(at + zi, SUB, stride=strips), :] = value[zi * SUB : (zi + 1) * SUB]
        totals[0] = totals[0] + value * value

    sweep(functools.partial(packed, one), factor_last)

    marks = marks_ref[...]
    places = lax.broadcasted_iota(jnp.int32, marks.shape, 1)
    count = jnp.sum(jnp.where(places == lax.axis_index("dev"), marks, 0), axis=1, keepdims=True)
    parity = jnp.sum(jnp.where(places == marks.shape[1] - 1, marks, 0), axis=1, keepdims=True)
    signed = (1.0 - 2.0 * parity.astype(jnp.float32)) / slots

    lane_sum = jnp.broadcast_to(jnp.sum(totals[0], axis=0, keepdims=True), (SUB, rows))
    mean_square = (lane_sum + pltpu.roll(lane_sum, slots, 1)) * (LEADING * LEADING / (2 * cells))
    slot_ids = lax.broadcasted_iota(jnp.int32, (SUB, rows), 1) % slots
    scale = jnp.where(slot_ids < count, LEADING * lax.rsqrt(mean_square + 1e-06), 0.0)[:1]

    wide = 9 * CHUNK
    for x in range(2):
        for start in range(0, half, wide):
            at = x * half + start
            rounded = (final[at : at + wide, :] * scale).astype(jnp.bfloat16)
            turned = lax.dot_general(eye, rounded, across, preferred_element_type=jnp.float32)
            rounded = turned.astype(jnp.bfloat16)
            squares = turned * turned
            for part in range(2):
                mine = slice(part * slots, (part + 1) * slots)
                to = slice(part * half + start, part * half + start + wide)
                filtered_ref[x * slots : (x + 1) * slots, to] = rounded[mine]
                halves_ref[x : x + 1, to] = jnp.sum(squares[mine], axis=0, keepdims=True) * signed

    groups = lax.axis_size("grp")
    me = lax.axis_index("grp")
    width = cells // groups
    room = kept_ref.shape[1] // (groups // 2)
    parts = [halves_ref[:, i * width : (i + 1) * width] for i in range(groups)]
    span = 1
    while span < groups:
        swapped = (me & span) != 0
        parts = [jnp.where(swapped, parts[j ^ span], parts[j]) for j in range(groups)]
        span *= 2
    kept_ref[...] = jnp.zeros(kept_ref.shape, jnp.float32)
    sent_ref[...] = jnp.zeros(sent_ref.shape, jnp.float32)
    for j in range(groups // 2):
        kept_ref[:, j * room : j * room + width] = parts[j]
        sent_ref[:, j * room : j * room + width] = parts[groups // 2 + j]


def make_eye():
    return pl.pallas_call(
        eye_kernel,
        out_shape=jax.ShapeDtypeStruct((CHUNK, CHUNK), jnp.bfloat16),
        out_specs=pl.BlockSpec(memory_space=pltpu.VMEM),
        compiler_params=pltpu.CompilerParams(vmem_limit_bytes=2**20),
        cost_estimate=pl.CostEstimate(flops=10**10, bytes_accessed=0, transcendentals=0),
        name="make_eye",
    )()


def turn_orbitals(orbitals, near, eye):
    slots, planes, cells = orbitals.shape
    vmem = pl.BlockSpec(memory_space=pltpu.VMEM)
    return pl.pallas_call(
        turn_kernel,
        out_shape=(
            jax.ShapeDtypeStruct((cells, planes * slots), jnp.float32),
            jax.ShapeDtypeStruct((cells // 2, planes * slots), jnp.float32),
        ),
        in_specs=[vmem] * 3,
        out_specs=(vmem, vmem),
        compiler_params=pltpu.CompilerParams(vmem_limit_bytes=8 * 2**20),
        name="turn_orbitals",
    )(orbitals, near, eye)


def filter_box(marks, plain, near_diagonal, far):
    cells, rows = plain.shape
    field, half = pltpu.VMEM((cells, rows), jnp.float32), pltpu.VMEM((cells // 2, rows), jnp.float32)
    vmem = pl.BlockSpec(memory_space=pltpu.VMEM)
    groups = lax.axis_size("grp")
    room = pl.cdiv(cells // groups, 128) * 128
    part = jax.ShapeDtypeStruct((2, groups // 2 * room), jnp.float32)
    return pl.pallas_call(
        filter_kernel,
        out_shape=(
            jax.ShapeDtypeStruct((rows, cells), jnp.bfloat16),
            part,
            part,
        ),
        in_specs=[vmem] * 4,
        out_specs=(vmem, vmem, vmem),
        scratch_shapes=[pltpu.VMEM((2, cells), jnp.float32), field, half, field, field, field],
        compiler_params=pltpu.CompilerParams(vmem_limit_bytes=16 * 2**20),
        name="filter_box",
    )(marks, plain, near_diagonal, far)


def sum_blocks(kept, sent, width):
    groups, devs = lax.axis_size("grp"), lax.axis_size("dev")
    span = groups // 2
    while span > 1:
        part = kept + lax.ppermute(sent, "grp", [(g, g ^ span) for g in range(groups)])
        half = part.shape[1] // 2
        kept, sent = part[:, :half], part[:, half:]
        span //= 2
    both_axes = ("grp", "dev")
    places = [(g, d) for g in range(groups) for d in range(devs)]
    carried = lax.ppermute(kept[1:], both_axes, [(g * devs + d, g * devs + (d + 1) % devs) for g, d in places])
    beside = lax.ppermute(sent[:1], both_axes, [(g * devs + d, (g ^ 1) * devs + d) for g, d in places])
    slanted = lax.ppermute(sent[1:], both_axes, [(g * devs + d, (g ^ 1) * devs + (d + 1) % devs) for g, d in places])
    return (kept[:1] + beside + carried + slanted)[:, :width]


def on_device(orbitals, potential, counts, parity):
    group_size = lax.axis_size("dev")
    slots, _, cells = orbitals.shape[2:]
    far = lax.ppermute(potential, "dev", [((i + 1) % group_size, i) for i in range(group_size)])
    marks = jnp.concatenate([counts, parity], 1)
    eye = make_eye()
    plain, near_diagonal = turn_orbitals(orbitals[0, 0], potential, eye)
    filtered_rows, kept, sent = filter_box(marks, plain, near_diagonal, far)
    density = sum_blocks(kept, sent, cells // lax.axis_size("grp"))
    filtered = jnp.swapaxes(filtered_rows.reshape(2, slots, cells), 0, 1)
    return density[None], filtered[None, None]


def solution(mesh):
    placed = (P("grp", "dev", None, None, None), P("dev", None), P("grp", None), P("grp", "dev"))
    return jax.shard_map(
        on_device,
        mesh=mesh,
        in_specs=placed,
        out_specs=(P("dev", None, "grp"), P("grp", "dev", None, None, None)),
        check_vma=False,
    )
```

```python
import functools
import math

import jax
import jax.numpy as jnp
from jax import lax
from jax.experimental import pallas as pl
from jax.experimental.pallas import tpu as pltpu
from jax.sharding import PartitionSpec as P

DEGREE = 8
BZ = 48
SUB = 8
CHUNK = 128

filter_centre = 9.0
filter_half = 7.0

across = (((1,), (1,)), ((), ()))


def leja_roots():
    rest = [math.cos((2 * j - 1) * math.pi / (2 * DEGREE)) for j in range(1, DEGREE + 1)]
    order = [rest.pop(0)]
    while rest:
        best = max(rest, key=lambda root: sum(math.log(abs(root - other)) for other in order))
        rest.remove(best)
        order.append(best)
    return order


SHIFTS = [filter_half * root + filter_centre - 6.0 for root in leja_roots()]
LEADING = 2.0 ** (DEGREE - 1) / filter_half**DEGREE


def identity(size):
    down = lax.broadcasted_iota(jnp.int32, (size, size), 0)
    along = lax.broadcasted_iota(jnp.int32, (size, size), 1)
    return (down == along).astype(jnp.float32).astype(jnp.bfloat16)


def eye_kernel(eye_ref):
    eye_ref[...] = identity(eye_ref.shape[0])


def half_rows(row_ref, start, slots):
    upper = row_ref.shape[1] // 2 + start
    return [
        jnp.broadcast_to(row_ref[0:1, at : at + CHUNK], (slots, CHUNK)) for at in (start, upper)
    ]


def turn_kernel(orbital_ref, near_ref, eye_ref, plain, near_diagonal):
    slots, _, cells = orbital_ref.shape
    half, rows = cells // 2, 2 * slots
    eye = eye_ref[...]
    for start in range(0, half, CHUNK):
        lower = jnp.swapaxes(orbital_ref[:, :, start : start + CHUNK], 0, 1)
        upper = jnp.swapaxes(orbital_ref[:, :, half + start : half + start + CHUNK], 0, 1)
        parts = [lower[0], upper[0], lower[1], upper[1]] + half_rows(near_ref, start, slots)
        turned = lax.dot_general(
            eye, jnp.concatenate(parts, 0), across, preferred_element_type=jnp.float32
        )
        plain[start : start + CHUNK, :] = turned[:, :rows]
        plain[half + start : half + start + CHUNK, :] = turned[:, rows : 2 * rows]
        near_diagonal[start : start + CHUNK, :] = turned[:, 2 * rows :]


def filter_kernel(
    marks_ref,
    plain,
    near_diagonal,
    far_ref,
    filtered_ref,
    kept_ref,
    sent_ref,
    halves_ref,
    ordered,
    far_diagonal,
    one,
    two,
    final,
):
    cells, rows = plain.shape
    slots, half = rows // 2, cells // 2
    strips = BZ // SUB
    height = half // BZ

    eye = identity(CHUNK)
    for start in range(0, half, CHUNK):
        potential = lax.dot_general(
            eye,
            jnp.concatenate(half_rows(far_ref, start, slots), 0),
            across,
            preferred_element_type=jnp.float32,
        )
        far_diagonal[start : start + CHUNK, :] = potential

    sub_ids = lax.broadcasted_iota(jnp.int32, (SUB, rows), 0)
    is_first, is_last = sub_ids == 0, sub_ids == SUB - 1
    is_lower = lax.broadcasted_iota(jnp.int32, (BZ, rows), 1) < slots

    def strided(ref, at):
        return jnp.concatenate(
            [ref[pl.ds(at + zi, SUB, stride=strips), :] for zi in range(strips)], 0
        )

    def packed(ref, at):
        return ref[at : at + BZ, :]

    def lowered(row):
        first = jnp.where(is_first, 0.0, pltpu.roll(row[BZ - SUB :], 1, 0))
        return jnp.concatenate([first, row[: BZ - SUB]], 0)

    def sweep(load, finish):
        here = [load(x * half) for x in range(2)]
        ends = [jnp.where(is_lower, pltpu.roll(row, slots, 1), 0.0) for row in here]
        before = [pltpu.roll(load(x * half + half - BZ), slots, 1) for x in range(2)]
        before = [jnp.where(is_lower, 0.0, row) for row in before]
        slanted = [row + lowered(last) for row, last in zip(here, before)]
        corner = [row[BZ - SUB :] for row in before]
        for y in range(height):
            after = [load(x * half + (y + 1) * BZ) if y + 1 < height else ends[x] for x in range(2)]
            for x in range(2):
                new = after[x] + lowered(here[x])
                upper = jnp.where(is_last, corner[x], pltpu.roll(slanted[x][:SUB], SUB - 1, 0))
                beside = new + jnp.concatenate([slanted[x][SUB:], upper], 0)
                finish(x, y * BZ, here[x], beside + here[1 - x])
                slanted[x] = new
            corner = [row[BZ - SUB :] for row in here]
            here = after

    def factor_first(x, at, here, beside):
        weight = strided((near_diagonal, far_diagonal)[x], at)
        at = x * half + at
        ordered[at : at + BZ, :] = weight
        one[at : at + BZ, :] = (weight - SHIFTS[0]) * here - beside

    sweep(functools.partial(strided, plain), factor_first)

    def pick(pair, shifts):
        shift = jnp.float32(shifts[0])
        for index, other in enumerate(shifts[1:], 1):
            shift = jnp.where(pair == index, jnp.float32(other), shift)
        return shift

    def factor_pair(pair, carry):
        for source, target, shifts in ((one, two, SHIFTS[1:-1:2]), (two, one, SHIFTS[2:-1:2])):
            shift = pick(pair, shifts)

            def factor(x, at, here, beside, target=target, shift=shift):
                at = x * half + at
                target[at : at + BZ, :] = (packed(ordered, at) - shift) * here - beside

            sweep(functools.partial(packed, source), factor)
        return carry

    lax.fori_loop(0, (DEGREE - 2) // 2, factor_pair, 0)

    totals = [jnp.zeros((BZ, rows), jnp.float32)]

    def factor_last(x, at, here, beside):
        at = x * half + at
        value = (packed(ordered, at) - SHIFTS[-1]) * here - beside
        for zi in range(strips):
            final[pl.ds(at + zi, SUB, stride=strips), :] = value[zi * SUB : (zi + 1) * SUB]
        totals[0] = totals[0] + value * value

    sweep(functools.partial(packed, one), factor_last)

    marks = marks_ref[...]
    places = lax.broadcasted_iota(jnp.int32, marks.shape, 1)
    count = jnp.sum(jnp.where(places == lax.axis_index("dev"), marks, 0), axis=1, keepdims=True)
    parity = jnp.sum(jnp.where(places == marks.shape[1] - 1, marks, 0), axis=1, keepdims=True)
    signed = (1.0 - 2.0 * parity.astype(jnp.float32)) / slots

    lane_sum = jnp.broadcast_to(jnp.sum(totals[0], axis=0, keepdims=True), (SUB, rows))
    mean_square = (lane_sum + pltpu.roll(lane_sum, slots, 1)) * (LEADING * LEADING / (2 * cells))
    slot_ids = lax.broadcasted_iota(jnp.int32, (SUB, rows), 1) % slots
    scale = jnp.where(slot_ids < count, LEADING * lax.rsqrt(mean_square + 1e-06), 0.0)[:1]

    wide = 9 * CHUNK
    for x in range(2):
        for start in range(0, half, wide):
            at = x * half + start
            rounded = (final[at : at + wide, :] * scale).astype(jnp.bfloat16)
            turned = lax.dot_general(eye, rounded, across, preferred_element_type=jnp.float32)
            rounded = turned.astype(jnp.bfloat16)
            squares = turned * turned
            for part in range(2):
                mine = slice(part * slots, (part + 1) * slots)
                to = slice(part * half + start, part * half + start + wide)
                filtered_ref[x * slots : (x + 1) * slots, to] = rounded[mine]
                halves_ref[x : x + 1, to] = jnp.sum(squares[mine], axis=0, keepdims=True) * signed

    groups = lax.axis_size("grp")
    me = lax.axis_index("grp")
    width = cells // groups
    room = kept_ref.shape[1] // (groups // 2)
    padding = jnp.zeros((2, room - width), jnp.float32)
    parts = [
        jnp.concatenate([halves_ref[:, i * width : (i + 1) * width], padding], 1) for i in range(groups)
    ]
    span = 1
    while span < groups:
        swapped = (me & span) != 0
        parts = [jnp.where(swapped, parts[j ^ span], parts[j]) for j in range(groups)]
        span *= 2
    for j in range(groups // 2):
        kept_ref[:, j * room : (j + 1) * room] = parts[j]
        sent_ref[:, j * room : (j + 1) * room] = parts[groups // 2 + j]


def make_eye():
    return pl.pallas_call(
        eye_kernel,
        out_shape=jax.ShapeDtypeStruct((CHUNK, CHUNK), jnp.bfloat16),
        out_specs=pl.BlockSpec(memory_space=pltpu.VMEM),
        compiler_params=pltpu.CompilerParams(vmem_limit_bytes=2**20),
        cost_estimate=pl.CostEstimate(flops=10**10, bytes_accessed=0, transcendentals=0),
        name="make_eye",
    )()


def turn_orbitals(orbitals, near, eye):
    slots, planes, cells = orbitals.shape
    vmem = pl.BlockSpec(memory_space=pltpu.VMEM)
    return pl.pallas_call(
        turn_kernel,
        out_shape=(
            jax.ShapeDtypeStruct((cells, planes * slots), jnp.float32),
            jax.ShapeDtypeStruct((cells // 2, planes * slots), jnp.float32),
        ),
        in_specs=[vmem] * 3,
        out_specs=(vmem, vmem),
        compiler_params=pltpu.CompilerParams(vmem_limit_bytes=8 * 2**20),
        name="turn_orbitals",
    )(orbitals, near, eye)


def filter_box(marks, plain, near_diagonal, far):
    cells, rows = plain.shape
    field, half = pltpu.VMEM((cells, rows), jnp.float32), pltpu.VMEM((cells // 2, rows), jnp.float32)
    vmem = pl.BlockSpec(memory_space=pltpu.VMEM)
    groups = lax.axis_size("grp")
    room = pl.cdiv(cells // groups, 128) * 128
    part = jax.ShapeDtypeStruct((2, groups // 2 * room), jnp.float32)
    return pl.pallas_call(
        filter_kernel,
        out_shape=(
            jax.ShapeDtypeStruct((rows, cells), jnp.bfloat16),
            part,
            part,
        ),
        in_specs=[vmem] * 4,
        out_specs=(vmem, vmem, vmem),
        scratch_shapes=[pltpu.VMEM((2, cells), jnp.float32), field, half, field, field, field],
        compiler_params=pltpu.CompilerParams(vmem_limit_bytes=16 * 2**20),
        name="filter_box",
    )(marks, plain, near_diagonal, far)


def sum_blocks(kept, sent, width):
    groups, devs = lax.axis_size("grp"), lax.axis_size("dev")
    span = groups // 2
    while span > 1:
        part = kept + lax.ppermute(sent, "grp", [(g, g ^ span) for g in range(groups)])
        half = part.shape[1] // 2
        kept, sent = part[:, :half], part[:, half:]
        span //= 2
    both_axes = ("grp", "dev")
    places = [(g, d) for g in range(groups) for d in range(devs)]
    carried = lax.ppermute(kept[1:], both_axes, [(g * devs + d, g * devs + (d + 1) % devs) for g, d in places])
    beside = lax.ppermute(sent[:1], both_axes, [(g * devs + d, (g ^ 1) * devs + d) for g, d in places])
    slanted = lax.ppermute(sent[1:], both_axes, [(g * devs + d, (g ^ 1) * devs + (d + 1) % devs) for g, d in places])
    return (kept[:1] + beside + carried + slanted)[:, :width]


def on_device(orbitals, potential, counts, parity):
    group_size = lax.axis_size("dev")
    slots, _, cells = orbitals.shape[2:]
    far = lax.ppermute(potential, "dev", [((i + 1) % group_size, i) for i in range(group_size)])
    marks = jnp.concatenate([counts, parity], 1)
    eye = make_eye()
    plain, near_diagonal = turn_orbitals(orbitals[0, 0], potential, eye)
    filtered_rows, kept, sent = filter_box(marks, plain, near_diagonal, far)
    density = sum_blocks(kept, sent, cells // lax.axis_size("grp"))
    filtered = jnp.swapaxes(filtered_rows.reshape(2, slots, cells), 0, 1)
    return density[None], filtered[None, None]


def solution(mesh):
    placed = (P("grp", "dev", None, None, None), P("dev", None), P("grp", None), P("grp", "dev"))
    return jax.shard_map(
        on_device,
        mesh=mesh,
        in_specs=placed,
        out_specs=(P("dev", None, "grp"), P("grp", "dev", None, None, None)),
        check_vma=False,
    )
```
